32 devices in a mesh: row: 8 (over z, y), col: 4 (over x, core).
Axes of the slice: x: 2, y: 2, z: 4, core: 2. Of those that a mesh axis runs over, the one named last changes fastest.
Arguments:
- points: float32 [8192, 64], P(('col', 'row')), may hold values from -6 to 6
- feature_scale: float32 [64], replicated, may hold values from 0.1 to 0.5
- test_matrix: bfloat16 [8192, 256], P(('col', 'row')), may hold values from -6 to 6
- targets: float32 [8192], P(('col', 'row')), may hold values from -6 to 6
- ridge: float32 [1], replicated, may hold values from 0.5 to 2
Outputs:
- coefficients: float32 [8192], P(('col', 'row'))
- residual: float32 [8192], P(('col', 'row'))
- sketch: float32 [8192, 256], P(('col', 'row'))
The draws below stay inside these ranges and needn't reach their ends.
All inputs are finite; a program needn't handle non-finite values.
Results may differ from the reference program's by a relative error of at most 0.012.
The reference program's roundings to bfloat16 on the way count: a program that leaves them out, or rounds other values in their place, can miss the bound.
Values may be sent and summed in bfloat16 or wider, within the bound.
A program may use at most 128 MiB of HBM per device.

```python
import math
import jax
import jax.numpy as jnp
from jax import lax

FEATURES = 64
RANK = 256
ITERS = 2
POINTS = 8192


def level_of(own_key, dims, pieces, least, top_value):
    loudness, own = 1.0, jax.random.fold_in(own_key, 6)
    for position, blocks in pieces:
        steps = jnp.exp(jax.random.uniform(jax.random.fold_in(own, position), (blocks,), jnp.float32, least / len(pieces), top_value / len(pieces)))
        loudness = loudness * jnp.repeat(steps, dims[position] // blocks).reshape([-1 if axis == position else 1 for axis in range(len(dims))])
    return loudness


def centred(stream_key, extent, deviation, reach, pieces=(), kind=jnp.bfloat16):
    entries = deviation * jax.random.normal(stream_key, extent, jnp.float32)
    if pieces:
        entries = entries * level_of(stream_key, extent, pieces, -0.22, 0.18)
    return jnp.clip(entries, -reach, reach).astype(kind)


def setup_inputs(seed: int = 0) -> dict:
    seeds = jax.random.split(jax.random.key(seed), 6)
    points = centred(seeds[0], (POINTS, FEATURES), 1.0, 6.0, ((0, 32),), jnp.float32)
    feature_scale = jnp.clip(jnp.exp(jax.random.uniform(seeds[1], (FEATURES,), jnp.float32, math.log(0.1), math.log(0.5))), 0.1, 0.5)
    test_matrix = centred(seeds[2], (POINTS, RANK), 1.0, 6.0, ((0, 32),))
    targets = centred(seeds[3], (POINTS,), 1.0, 6.0, ((0, 32),), jnp.float32)
    ridge = jnp.clip(jnp.exp(jax.random.uniform(seeds[4], (1,), jnp.float32, math.log(0.5), math.log(2.0))), 0.5, 2.0)
    return dict(points=points, feature_scale=feature_scale, test_matrix=test_matrix, targets=targets, ridge=ridge)


def kernel_block(left, left_norm, right, right_norm):
    cross = lax.dot_general(left.astype(jnp.float32), right.astype(jnp.float32), (((1,), (1,)), ((), ())), precision=lax.Precision.HIGHEST, preferred_element_type=jnp.float32)
    return jnp.exp(-0.5 * (left_norm[:, None] + right_norm[None, :] - 2.0 * cross))

def core_solve(lower, vector):
    middle = lax.linalg.triangular_solve(lower, vector[:, None], left_side=True, lower=True)
    return lax.linalg.triangular_solve(lower, middle, left_side=True, lower=True, transpose_a=True)[:, 0]

def reference(points, feature_scale, test_matrix, targets, ridge):
    ridge_value = ridge[0]
    scaled = points * feature_scale[None, :]
    norms = jnp.sum(scaled * scaled, axis=1)
    block_rows = math.gcd(POINTS, 512)
    blocks = POINTS // block_rows
    scaled_blocks = scaled.reshape(blocks, block_rows, FEATURES)
    norm_blocks = norms.reshape(blocks, block_rows)
    test_wide = test_matrix.astype(jnp.float32)

    def sketch_rows(pair):
        weights = kernel_block(pair[0], pair[1], scaled, norms).astype(jnp.bfloat16)
        weights = lax.optimization_barrier(weights).astype(jnp.float32)
        return jnp.dot(weights.astype(jnp.float32), test_wide.astype(jnp.float32), precision=lax.Precision.HIGHEST, preferred_element_type=jnp.float32)
    sketch = lax.map(sketch_rows, (scaled_blocks, norm_blocks)).reshape(POINTS, RANK)

    def operate(vector):

        def rows_term(pair):
            weights = kernel_block(pair[0], pair[1], scaled, norms)
            return jnp.dot(weights.astype(jnp.float32), vector.astype(jnp.float32), precision=lax.Precision.HIGHEST, preferred_element_type=jnp.float32)
        return lax.map(rows_term, (scaled_blocks, norm_blocks)).reshape(POINTS) + ridge_value * vector
    gram_test = lax.dot_general(test_wide.astype(jnp.float32), sketch.astype(jnp.float32), (((0,), (0,)), ((), ())), precision=lax.Precision.HIGHEST, preferred_element_type=jnp.float32)
    gram_sketch = lax.dot_general(sketch.astype(jnp.float32), sketch.astype(jnp.float32), (((0,), (0,)), ((), ())), precision=lax.Precision.HIGHEST, preferred_element_type=jnp.float32)
    lower = jnp.linalg.cholesky(ridge_value * gram_test + gram_sketch)

    def precondition(resid):
        projected = jnp.dot(resid.astype(jnp.float32), sketch.astype(jnp.float32), precision=lax.Precision.HIGHEST, preferred_element_type=jnp.float32)
        solved = core_solve(lower, projected)
        return (resid - jnp.dot(sketch.astype(jnp.float32), solved.astype(jnp.float32), precision=lax.Precision.HIGHEST, preferred_element_type=jnp.float32)) / ridge_value
    coefficients = jnp.zeros((POINTS,), jnp.float32)
    resid = targets
    precond = precondition(resid)
    descent = jnp.sum(resid * precond)
    direction = precond
    for turn in range(ITERS):
        image = operate(direction)
        step_size = descent / jnp.sum(direction * image)
        coefficients = coefficients + step_size * direction
        if turn + 1 < ITERS:
            resid = resid - step_size * image
            precond = precondition(resid)
            fresh = jnp.sum(resid * precond)
            direction = precond + fresh / descent * direction
            descent = fresh
    residual = targets - operate(coefficients)
    return (coefficients, residual, sketch)
```

```python
import functools

import jax
import jax.numpy as jnp
from jax import lax
from jax.experimental import pallas as pl
from jax.experimental.pallas import tpu as pltpu
from jax.sharding import PartitionSpec as P

MESH = pl.DeviceIdType.MESH
EXACT = lax.Precision.HIGHEST
NN = (((1,), (0,)), ((), ()))
NT = (((1,), (1,)), ((), ()))
TN = (((0,), (0,)), ((), ()))
X_COL, PAIR, SKETCH, CORE, CORE_ROW, CORE_ALL, CORE_COL, W_ROW, W_COL = range(9)
Z_ROW, Q_COL, A_ROW, A_COL = (9, 13), (10, 14), (11, 15), (12, 16)
ROUNDS = 17
CORES = 2


def exact(left, right, dims):
    return lax.dot_general(
        left, right, dims, precision=EXACT, preferred_element_type=jnp.float32
    )


def invert(a):
    size, width = a.shape[0], 4
    lane = lax.broadcasted_iota(jnp.int32, a.shape, 1)
    lane_row = lane[0:1, :]

    def pivots(a, k):
        entry = [
            [jnp.broadcast_to(a[k + i : k + i + 1, k + j : k + j + 1], (1, size)) for j in range(width)]
            for i in range(width)
        ]
        rows = [a[k + i : k + i + 1, :] for i in range(width)]
        cols = [a[:, k + i : k + i + 1] for i in range(width)]
        for t in range(width):
            inverse = 1.0 / entry[t][t]
            here = lane_row == k + t
            rows[t] = jnp.where(here, inverse, rows[t] * inverse)
            for j in range(t + 1, width):
                entry[t][j] = entry[t][j] * inverse
            for i in range(width):
                if i != t:
                    factor = entry[i][t]
                    rows[i] = jnp.where(here, 0.0, rows[i]) - factor * rows[t]
                    for j in range(t + 1, width):
                        entry[i][j] = entry[i][j] - factor * entry[t][j]
        out = jnp.where((lane >= k) & (lane < k + width), 0.0, a)
        for t in range(width):
            out = out - cols[t] * rows[t]
        return out, rows

    def turn(_, a):
        a, upper = pivots(a, 0)
        a = jnp.concatenate(upper + [a[width:, :]], axis=0)
        a, lower = pivots(a, width)
        a = jnp.concatenate([a[8:, :], a[:width, :]] + lower, axis=0)
        return pltpu.roll(a, size - 8, 1)

    return lax.fori_loop(0, size // 8, turn, a)


def kernel(
    R, C, pts, scale, test, tgt, ridge, coef_out, resid_out, sketch_out,
    xrow, trow, xcol, left, left_norm, kmat, part, pair, srecv, core, crecv, crow, cgath, call, inv,
    vrow, vcol, qpart, qcol, send, recv, gather_send, gather_recv,
):
    r, c = lax.axis_index("row"), lax.axis_index("col")
    n, feats = pts.shape
    rank = test.shape[1]
    chunk = rank // C
    piece = chunk // R
    B = R // 4 if R % 4 == 0 else 1
    A = R // B
    half = rank // 2
    lam = ridge[0, 0]

    def to_row(i):
        return (lax.rem(r + i, R), c)

    def to_col(i):
        return (r, lax.rem(c + i, C))

    def copy(src, dst, out, into, dev):
        return pltpu.make_async_remote_copy(
            src_ref=src, dst_ref=dst, send_sem=out, recv_sem=into,
            device_id=dev, device_id_type=MESH,
        )

    def push(src, dst, k, dev):
        copy(src, dst, send.at[k], recv.at[k], dev).start()

    def spread_row(buf, k):
        for i in range(1, R):
            push(buf.at[r], buf.at[r], k, to_row(i))

    def spread_col(buf, k):
        for i in range(1, C):
            push(buf.at[c], buf.at[c], k, to_col(i))

    def arrived(buf, k):
        part_of = buf.at[pl.ds(0, buf.shape[0] - 1)]
        pltpu.make_async_copy(part_of, part_of, recv.at[k]).wait()

    def sent(buf, k):
        part_of = buf.at[pl.ds(0, buf.shape[0] - 1)]
        pltpu.make_async_copy(part_of, part_of, send.at[k]).wait()

    def total(buf):
        acc = buf[0]
        for i in range(1, buf.shape[0]):
            acc = acc + buf[i]
        return acc

    barrier = pltpu.get_barrier_semaphore()
    for i in range(1, R):
        pl.semaphore_signal(barrier, inc=1, device_id=to_row(i), device_id_type=MESH)
    for i in range(1, C):
        pl.semaphore_signal(barrier, inc=1, device_id=to_col(i), device_id_type=MESH)

    scaled = pts[...] * scale[...]
    high = scaled.astype(jnp.bfloat16).astype(jnp.float32)
    both = jnp.concatenate([high, scaled - high], axis=1).astype(jnp.bfloat16)
    xrow[r] = both
    xcol[c] = both
    trow[r] = test[...]
    pl.semaphore_wait(barrier, R + C - 2)
    spread_col(xcol, X_COL)

    along, across = lax.div(r, B), lax.rem(r, B)
    stores = (xrow, trow)

    def hops(slot, s):
        origin = lax.div(slot, B)

        def make(kind, dev):
            return copy(
                stores[s].at[slot], stores[s].at[slot], gather_send.at[s, slot, kind],
                gather_recv.at[s, slot], (dev, c),
            )

        out = [
            ((origin <= along) & (along + 1 < A), make(0, lax.rem(r + B, R))),
            ((origin >= along) & (along >= 1), make(1, lax.rem(r + R - B, R))),
        ]
        for i in range(1, B):
            out.append((None, make(1 + i, along * B + lax.rem(across + i, B))))
        return out

    def forward(slot, s):
        for condition, move in hops(slot, s):
            if condition is None:
                move.start()
            else:
                pl.when(condition)(move.start)

    def landed(slot, s):
        here = stores[s].at[slot]
        pltpu.make_async_copy(here, here, gather_recv.at[s, slot]).wait()

    ones = jnp.ones((8, 128), jnp.float32)

    def pair_sum(x):
        swapped = pltpu.roll(x, feats, 1)
        return swapped, x * (x + swapped)

    def consume(slot, first=False):
        y = xrow[slot]
        right_norm = -0.5 * exact(ones, pair_sum(y.astype(jnp.float32))[1], NT)[0:1, :]
        right = jnp.concatenate([y, y], axis=1)

        def block(m, carry):
            cross = lax.dot_general(left[m], right, NT, preferred_element_type=jnp.float32)
            norm = left_norm[m]
            weights = jnp.exp(cross + jnp.concatenate([norm] * (n // 128), axis=1) + right_norm)
            kmat[slot, m] = weights
            term = lax.dot_general(
                weights.astype(jnp.bfloat16), trow[slot], NN, preferred_element_type=jnp.float32
            )
            part[m] = term if first else part[m] + term
            return carry

        lax.fori_loop(0, C, block, 0)

    def line(d):
        return ((along >= d, r - d * B), (along + d < A, r + d * B))

    for s in range(2):
        forward(r, s)
    arrived(xcol, X_COL)
    for m in range(C):
        x = xcol[m]
        swapped, square = pair_sum(x.astype(jnp.float32))
        left[m] = jnp.concatenate([x, swapped.astype(jnp.bfloat16)], axis=1)
        left_norm[m] = jnp.broadcast_to(-0.5 * jnp.sum(square, axis=1, keepdims=True), (n, 128))
    consume(r, first=True)
    for d in range(1, A):
        for s in range(2):
            for there, slot in line(d):

                @pl.when(there)
                def _(slot=slot, s=s):
                    landed(slot, s)
                    forward(slot, s)

        for there, slot in line(d):
            pl.when(there)(functools.partial(consume, slot))
    for i in range(1, B):
        other = along * B + lax.rem(across + i, B)
        for d in range(A):
            for there, slot in line(d) if d else ((None, r),):
                slot = slot - r + other

                def use(slot=slot):
                    landed(slot, 0)
                    landed(slot, 1)
                    consume(slot)

                if there is None:
                    use()
                else:
                    pl.when(there)(use)

    chip, side = lax.div(c, CORES), lax.rem(c, CORES)
    chips = C // CORES
    for i in range(chips):
        m = lax.rem(chip + 1 + i, chips) * CORES + 1 - side
        push(part.at[m], pair.at[m - 1 + side], PAIR, (r, chip * CORES + 1 - side))
    mine = pair.at[pl.ds(0, chips)]
    pltpu.make_async_copy(mine, mine, recv.at[PAIR]).wait()
    for i in range(chips):
        m = lax.rem(chip + 1 + i, chips)
        summed = part[m * CORES + side] + pair[m * CORES]
        if i < chips - 1:
            part[m * CORES + side] = summed
            push(part.at[m * CORES + side], srecv.at[chip], SKETCH, (r, m * CORES + side))
        else:
            srecv[chip] = summed
    arrived(srecv, SKETCH)
    sketch = total(srecv)
    sketch_out[...] = sketch

    resid = jnp.broadcast_to(tgt[...], (8, n))
    local = exact(lam * test[...].astype(jnp.float32) + sketch, sketch, TN)
    for i in range(C):
        core[i] = local[i * chunk : (i + 1) * chunk, :]
    for i in range(1, C):
        push(core.at[lax.rem(c + i, C)], crecv.at[c], CORE, to_col(i))
    w_row, w_col = vrow.at[0], vcol.at[0]
    w_row[r, :, 0:rank] = exact(resid, sketch, NN)[0:1, :]
    w_row[r, :, rank : rank + 128] = jnp.zeros((1, 128), jnp.float32)
    spread_row(w_row, W_ROW)
    crecv[c] = core[c]
    arrived(crecv, CORE)
    summed = total(crecv)
    for i in range(R):
        crow[0, i] = summed[i * piece : (i + 1) * piece, :]
    for i in range(1, R):
        push(crow.at[0, lax.rem(r + i, R)], crow.at[1, r], CORE_ROW, to_row(i))
    arrived(w_row, W_ROW)
    w_col[c] = total(w_row)
    spread_col(w_col, W_COL)
    crow[1, r] = crow[0, r]
    arrived(crow.at[1], CORE_ROW)
    cgath[r] = total(crow.at[1])
    spread_row(cgath, CORE_ALL)
    arrived(cgath, CORE_ALL)
    call[c] = cgath[...].reshape(chunk, rank)
    spread_col(call, CORE_COL)
    arrived(w_col, W_COL)
    w = total(w_col)[:, 0:rank]
    arrived(call, CORE_COL)

    whole = call[...].reshape(rank, rank)
    top, up = whole[:half, :half], whole[:half, half:]
    down, low = whole[half:, :half], whole[half:, half:]
    first = invert(top)
    above = exact(first, up, NN)
    below = exact(down, first, NN)
    second = invert(low - exact(down, above, NN))
    corner = exact(second, below, NN)
    inv[:half, :half] = first + exact(above, corner, NN)
    inv[:half, half:] = -exact(above, second, NN)
    inv[half:, :half] = -corner
    inv[half:, half:] = second

    def lanes(x):
        return jnp.sum(x, axis=1, keepdims=True)

    def wide(x):
        return jnp.broadcast_to(x[0:1, :], (1, 128))

    def precondition(resid, w):
        solved = exact(jnp.broadcast_to(w, (8, rank)), inv[...], NN)
        return (resid - exact(solved, sketch_out[...], NT)) / lam

    def operate(vector, inner, k):
        vec, sums = vrow.at[1 + 2 * k], qcol.at[k]
        vec[r, :, 0:n] = vector[0:1, :]
        vec[r, :, n : n + 128] = wide(lanes(inner))
        spread_row(vec, Z_ROW[k])
        arrived(vec, Z_ROW[k])
        inner_sum = total(vec)[:, n : n + 128]
        pieces = [vec[j] for j in range(R)]

        def block(i, carry):
            m = lax.rem(c + i, C)
            acc = jnp.zeros((n, 128), jnp.float32)
            for j in range(R):
                for h in range(0, n, 128):
                    acc += kmat[j, m, :, h : h + 128] * pieces[j][:, h : h + 128]
            qpart[k, m, :, 0:n] = exact(ones, acc, NT)[0:1, :]
            qpart[k, m, :, n : n + 128] = inner_sum

            @pl.when(i < C)
            def _():
                push(qpart.at[k, m], sums.at[c], Q_COL[k], (r, m))

            return carry

        lax.fori_loop(1, C + 1, block, 0)
        sums[c] = qpart[k, c]
        arrived(sums, Q_COL[k])
        out = total(sums)
        return out[:, 0:n] + lam * vector, out[:, n : n + 1]

    def reduce_all(row, scalar, k):
        across, along = vrow.at[2 + 2 * k], vcol.at[1 + k]
        across[r, :, 0:rank] = row[0:1, :]
        across[r, :, rank : rank + 128] = wide(scalar)
        spread_row(across, A_ROW[k])
        arrived(across, A_ROW[k])
        along[c] = total(across)
        spread_col(along, A_COL[k])
        arrived(along, A_COL[k])
        out = total(along)
        return out[:, 0:rank], out[:, rank : rank + 1]

    direction = precondition(resid, w)
    image, descent = operate(direction, resid * direction, 0)
    projected, curve = reduce_all(exact(image, sketch_out[...], NN), lanes(direction * image), 0)
    step = descent / curve
    coef = step * direction
    resid = resid - step * image
    precond = precondition(resid, w - step * projected)
    next_image, fresh = operate(precond, resid * precond, 1)
    ratio = fresh / descent
    direction = precond + ratio * direction
    image = next_image + ratio * image
    _, curve = reduce_all(direction, lanes(direction * image), 1)
    step = fresh / curve
    coef_out[...] = (coef + step * direction)[0:1, :]
    resid_out[...] = (resid - step * image)[0:1, :]

    for s in range(2):
        for d in range(A):
            for there, slot in line(d) if d else ((None, r),):
                for condition, move in hops(slot, s):
                    both = [x for x in (there, condition) if x is not None]
                    if both:
                        pl.when(functools.reduce(jnp.logical_and, both))(move.wait_send)
                    else:
                        move.wait_send()
    sent(xcol, X_COL)
    pltpu.make_async_copy(mine, mine, send.at[PAIR]).wait()
    sent(srecv, SKETCH)
    sent(crecv, CORE)
    sent(crow.at[1], CORE_ROW)
    sent(cgath, CORE_ALL)
    sent(call, CORE_COL)
    sent(w_row, W_ROW)
    sent(w_col, W_COL)
    for k in range(2):
        sent(vrow.at[1 + 2 * k], Z_ROW[k])
        sent(qcol.at[k], Q_COL[k])
        sent(vrow.at[2 + 2 * k], A_ROW[k])
        sent(vcol.at[1 + k], A_COL[k])


def local(R, C, points, feature_scale, test_matrix, targets, ridge):
    n, feats = points.shape
    rank = test_matrix.shape[1]
    f32, half = jnp.float32, jnp.bfloat16
    vmem = pl.BlockSpec(memory_space=pltpu.VMEM)
    coef, resid, sketch = pl.pallas_call(
        functools.partial(kernel, R, C),
        out_shape=(
            jax.ShapeDtypeStruct((1, n), f32),
            jax.ShapeDtypeStruct((1, n), f32),
            jax.ShapeDtypeStruct((n, rank), f32),
        ),
        in_specs=[vmem, vmem, vmem, vmem, pl.BlockSpec(memory_space=pltpu.SMEM)],
        out_specs=(vmem, vmem, vmem),
        scratch_shapes=[
            pltpu.VMEM((R, n, 2 * feats), half),
            pltpu.VMEM((R, n, rank), half),
            pltpu.VMEM((C, n, 2 * feats), half),
            pltpu.VMEM((C, n, 4 * feats), half),
            pltpu.VMEM((C, n, 128), f32),
            pltpu.VMEM((R, C, n, n), f32),
            pltpu.VMEM((C, n, rank), f32),
            pltpu.VMEM((C, n, rank), f32),
            pltpu.VMEM((C // CORES, n, rank), f32),
            pltpu.VMEM((C, rank // C, rank), f32),
            pltpu.VMEM((C, rank // C, rank), f32),
            pltpu.VMEM((2, R, rank // C // R, rank), f32),
            pltpu.VMEM((R, rank // C // R, rank), f32),
            pltpu.VMEM((C, rank // C, rank), f32),
            pltpu.VMEM((rank, rank), f32),
            pltpu.VMEM((5, R, 1, n + 128), f32),
            pltpu.VMEM((3, C, 1, n + 128), f32),
            pltpu.VMEM((2, C, 1, n + 128), f32),
            pltpu.VMEM((2, C, 1, n + 128), f32),
            pltpu.SemaphoreType.DMA((ROUNDS,)),
            pltpu.SemaphoreType.DMA((ROUNDS,)),
            pltpu.SemaphoreType.DMA((2, R, 6)),
            pltpu.SemaphoreType.DMA((2, R)),
        ],
        compiler_params=pltpu.CompilerParams(
            collective_id=0, has_side_effects=True, vmem_limit_bytes=56 * 1024 * 1024
        ),
    )(points, feature_scale.reshape(1, feats), test_matrix, targets.reshape(1, n), ridge.reshape(1, 1))
    return coef.reshape(n), resid.reshape(n), sketch


def solution(mesh):
    R, C = mesh.shape["row"], mesh.shape["col"]
    in_specs = (P(("col", "row"), None), P(), P(("col", "row"), None), P(("col", "row")), P())
    out_specs = (P(("col", "row")), P(("col", "row")), P(("col", "row"), None))
    return jax.shard_map(
        functools.partial(local, R, C), mesh=mesh, in_specs=in_specs, out_specs=out_specs,
        check_vma=False,
    )
```

```python
import functools

import jax
import jax.numpy as jnp
from jax import lax
from jax.experimental import pallas as pl
from jax.experimental.pallas import tpu as pltpu
from jax.sharding import PartitionSpec as P

MESH = pl.DeviceIdType.MESH
EXACT = lax.Precision.HIGHEST
NN = (((1,), (0,)), ((), ()))
NT = (((1,), (1,)), ((), ()))
TN = (((0,), (0,)), ((), ()))
X_COL, PAIR, SKETCH, CORE, CORE_ROW, CORE_ALL, CORE_COL, W_ROW, W_COL = range(9)
Z_ROW, Q_COL, A_ROW, A_COL = (9, 13), (10, 14), (11, 15), (12, 16)
ROUNDS = 17
CORES = 2


def exact(left, right, dims):
    return lax.dot_general(
        left, right, dims, precision=EXACT, preferred_element_type=jnp.float32
    )


def invert(a):
    size, width = a.shape[0], 4
    lane = lax.broadcasted_iota(jnp.int32, a.shape, 1)
    lane_row = lane[0:1, :]

    def pivots(a, k):
        entry = [
            [jnp.broadcast_to(a[k + i : k + i + 1, k + j : k + j + 1], (1, size)) for j in range(width)]
            for i in range(width)
        ]
        rows = [a[k + i : k + i + 1, :] for i in range(width)]
        cols = [a[:, k + i : k + i + 1] for i in range(width)]
        for t in range(0, width, 2):
            p, q, s, u = entry[t][t], entry[t][t + 1], entry[t + 1][t], entry[t + 1][t + 1]
            inverse = 1.0 / (p * u - q * s)
            p, q, s, u = u * inverse, -q * inverse, -s * inverse, p * inverse
            here, next_one = lane_row == k + t, lane_row == k + t + 1
            pair = here | next_one
            one, two = rows[t], rows[t + 1]
            rows[t] = jnp.where(here, p, jnp.where(next_one, q, p * one + q * two))
            rows[t + 1] = jnp.where(here, s, jnp.where(next_one, u, s * one + u * two))
            for j in range(t + 2, width):
                one, two = entry[t][j], entry[t + 1][j]
                entry[t][j], entry[t + 1][j] = p * one + q * two, s * one + u * two
            for i in range(width):
                if i not in (t, t + 1):
                    one, two = entry[i][t], entry[i][t + 1]
                    rows[i] = jnp.where(pair, 0.0, rows[i]) - one * rows[t] - two * rows[t + 1]
                    for j in range(t + 2, width):
                        entry[i][j] = entry[i][j] - one * entry[t][j] - two * entry[t + 1][j]
        out = jnp.where((lane >= k) & (lane < k + width), 0.0, a)
        for t in range(width):
            out = out - cols[t] * rows[t]
        return out, rows

    def turn(_, a):
        a, upper = pivots(a, 0)
        a = jnp.concatenate(upper + [a[width:, :]], axis=0)
        a, lower = pivots(a, width)
        a = jnp.concatenate([a[8:, :], a[:width, :]] + lower, axis=0)
        return pltpu.roll(a, size - 8, 1)

    return lax.fori_loop(0, size // 8, turn, a)


def kernel(
    R, C, pts, scale, test, tgt, ridge, coef_out, resid_out, sketch_out,
    xrow, trow, xcol, left, left_norm, kmat, part, pair, srecv, core, crecv, crow, cgath, call, inv, spread_ref,
    vrow, vcol, qpart, qcol, send, recv, gather_send, gather_recv,
):
    r, c = lax.axis_index("row"), lax.axis_index("col")
    feats, n = pts.shape
    rank = test.shape[1]
    chunk = rank // C
    piece = chunk // R
    B = R // 4 if R % 4 == 0 else 1
    A = R // B
    half = rank // 2
    lam = ridge[0, 0]

    def to_row(i):
        return (lax.rem(r + i, R), c)

    def to_col(i):
        return (r, lax.rem(c + i, C))

    def copy(src, dst, out, into, dev):
        return pltpu.make_async_remote_copy(
            src_ref=src, dst_ref=dst, send_sem=out, recv_sem=into,
            device_id=dev, device_id_type=MESH,
        )

    def push(src, dst, k, dev):
        copy(src, dst, send.at[k], recv.at[k], dev).start()

    def spread_row(buf, k):
        for i in range(1, R):
            push(buf.at[r], buf.at[r], k, to_row(i))

    def spread_col(buf, k):
        for i in range(1, C):
            push(buf.at[c], buf.at[c], k, to_col(i))

    def arrived(buf, k):
        part_of = buf.at[pl.ds(0, buf.shape[0] - 1)]
        pltpu.make_async_copy(part_of, part_of, recv.at[k]).wait()

    def sent(buf, k):
        part_of = buf.at[pl.ds(0, buf.shape[0] - 1)]
        pltpu.make_async_copy(part_of, part_of, send.at[k]).wait()

    def total(buf):
        acc = buf[0]
        for i in range(1, buf.shape[0]):
            acc = acc + buf[i]
        return acc

    barrier = pltpu.get_barrier_semaphore()
    for i in range(1, R):
        pl.semaphore_signal(barrier, inc=1, device_id=to_row(i), device_id_type=MESH)
    for i in range(1, C):
        pl.semaphore_signal(barrier, inc=1, device_id=to_col(i), device_id_type=MESH)

    scaled = pts[...].T * scale[...]
    high = scaled.astype(jnp.bfloat16).astype(jnp.float32)
    both = jnp.concatenate([high, scaled - high], axis=1).astype(jnp.bfloat16)
    xrow[r] = both
    xcol[c] = both
    trow[r] = test[...]
    part[...] = jnp.zeros_like(part)
    pl.semaphore_wait(barrier, R + C - 2)
    spread_col(xcol, X_COL)

    along, across = lax.div(r, B), lax.rem(r, B)
    stores = (xrow, trow)

    def hops(slot, s):
        origin = lax.div(slot, B)

        def make(kind, dev):
            return copy(
                stores[s].at[slot], stores[s].at[slot], gather_send.at[s, slot, kind],
                gather_recv.at[s, slot], (dev, c),
            )

        out = [
            ((origin <= along) & (along + 1 < A), make(0, lax.rem(r + B, R))),
            ((origin >= along) & (along >= 1), make(1, lax.rem(r + R - B, R))),
        ]
        for i in range(1, B):
            out.append((None, make(1 + i, along * B + lax.rem(across + i, B))))
        return out

    def forward(slot, s):
        for condition, move in hops(slot, s):
            if condition is None:
                move.start()
            else:
                pl.when(condition)(move.start)

    def landed(slot, s):
        here = stores[s].at[slot]
        pltpu.make_async_copy(here, here, gather_recv.at[s, slot]).wait()

    ones = jnp.ones((8, 128), jnp.float32)

    def pair_sum(x):
        swapped = pltpu.roll(x, feats, 1)
        return swapped, x * (x + swapped)

    def consume(slot):
        y = xrow[slot]
        right_norm = -0.5 * exact(ones, pair_sum(y.astype(jnp.float32))[1], NT)[0:1, :]
        cross = lax.dot_general(
            left[...].reshape(C * n, 4 * feats), jnp.concatenate([y, y], axis=1), NT,
            preferred_element_type=jnp.float32,
        )
        norm = left_norm[...].reshape(C * n, 128)
        weights = jnp.exp(cross + jnp.concatenate([norm] * (n // 128), axis=1) + right_norm)
        kmat[slot] = weights.reshape(C, n, n)
        term = lax.dot_general(
            weights.astype(jnp.bfloat16), trow[slot], NN, preferred_element_type=jnp.float32
        )
        part[...] = part[...] + term.reshape(C, n, rank)

    def line(d):
        return ((along >= d, r - d * B), (along + d < A, r + d * B))

    for s in range(2):
        forward(r, s)
    arrived(xcol, X_COL)
    for m in range(C):
        x = xcol[m]
        swapped, square = pair_sum(x.astype(jnp.float32))
        left[m] = jnp.concatenate([x, swapped.astype(jnp.bfloat16)], axis=1)
        left_norm[m] = jnp.broadcast_to(-0.5 * jnp.sum(square, axis=1, keepdims=True), (n, 128))

    def visit(t, carry):
        turn, place = lax.div(t, 2 * A - 1), lax.rem(t, 2 * A - 1)
        position = along + lax.div(place + 1, 2) * (1 - 2 * lax.rem(place, 2))

        @pl.when((position >= 0) & (position < A))
        def _():
            slot = position * B + lax.rem(across + turn, B)
            for s in range(2):

                @pl.when(t > 0)
                def _(s=s):
                    landed(slot, s)

                @pl.when((t > 0) & (turn == 0))
                def _(s=s):
                    forward(slot, s)

            consume(slot)

        return carry

    lax.fori_loop(0, B * (2 * A - 1), visit, 0)

    chip, side = lax.div(c, CORES), lax.rem(c, CORES)
    chips = C // CORES
    for i in range(chips):
        m = lax.rem(chip + 1 + i, chips) * CORES + 1 - side
        push(part.at[m], pair.at[m - 1 + side], PAIR, (r, chip * CORES + 1 - side))
    mine = pair.at[pl.ds(0, chips)]
    pltpu.make_async_copy(mine, mine, recv.at[PAIR]).wait()
    for i in range(chips):
        m = lax.rem(chip + 1 + i, chips)
        summed = part[m * CORES + side] + pair[m * CORES]
        if i < chips - 1:
            part[m * CORES + side] = summed
            push(part.at[m * CORES + side], srecv.at[chip], SKETCH, (r, m * CORES + side))
        else:
            srecv[chip] = summed
    arrived(srecv, SKETCH)
    sketch = total(srecv)
    sketch_out[...] = sketch

    resid = jnp.broadcast_to(tgt[...], (8, n))
    local = exact(lam * test[...].astype(jnp.float32) + sketch, sketch, TN)
    for i in range(C):
        core[i] = local[i * chunk : (i + 1) * chunk, :]
    for i in range(1, C):
        push(core.at[lax.rem(c + i, C)], crecv.at[c], CORE, to_col(i))
    w_row, w_col = vrow.at[0], vcol.at[0]
    w_row[r, :, 0:rank] = exact(resid, sketch, NN)[0:1, :]
    w_row[r, :, rank : rank + 128] = jnp.zeros((1, 128), jnp.float32)
    spread_row(w_row, W_ROW)
    crecv[c] = core[c]
    arrived(crecv, CORE)
    summed = total(crecv)
    for i in range(R):
        crow[0, i] = summed[i * piece : (i + 1) * piece, :]
    for i in range(1, R):
        push(crow.at[0, lax.rem(r + i, R)], crow.at[1, r], CORE_ROW, to_row(i))
    arrived(w_row, W_ROW)
    w_col[c] = total(w_row)
    spread_col(w_col, W_COL)
    crow[1, r] = crow[0, r]
    arrived(crow.at[1], CORE_ROW)
    cgath[r] = total(crow.at[1])
    spread_row(cgath, CORE_ALL)
    arrived(cgath, CORE_ALL)
    call[c] = cgath[...].reshape(chunk, rank)
    spread_col(call, CORE_COL)
    arrived(w_col, W_COL)
    w = total(w_col)[:, 0:rank]
    arrived(call, CORE_COL)

    whole = call[...].reshape(rank, rank)
    top, up = whole[:half, :half], whole[:half, half:]
    down, low = whole[half:, :half], whole[half:, half:]
    first = invert(top)
    above = exact(first, up, NN)
    below = exact(down, first, NN)
    second = invert(low - exact(down, above, NN))
    corner = exact(second, below, NN)
    inv[:half, :half] = first + exact(above, corner, NN)
    inv[:half, half:] = -exact(above, second, NN)
    inv[half:, :half] = -corner
    inv[half:, half:] = second

    spread_ref[...] = exact(inv[...], sketch, NT)

    def lanes(x):
        return jnp.sum(x, axis=1, keepdims=True)

    def wide(x):
        return jnp.broadcast_to(x[0:1, :], (1, 128))

    def precondition(resid, w):
        return (resid - exact(jnp.broadcast_to(w, (8, rank)), spread_ref[...], NN)) / lam

    def operate(vector, inner, k):
        vec, sums = vrow.at[1 + 2 * k], qcol.at[k]
        vec[r, :, 0:n] = vector[0:1, :]
        vec[r, :, n : n + 128] = wide(lanes(inner))
        spread_row(vec, Z_ROW[k])
        arrived(vec, Z_ROW[k])
        inner_sum = total(vec)[:, n : n + 128]
        pieces = [vec[j] for j in range(R)]

        def block(i, carry):
            m = lax.rem(c + i, C)
            acc = jnp.zeros((n, 128), jnp.float32)
            for j in range(R):
                for h in range(0, n, 128):
                    acc += kmat[j, m, :, h : h + 128] * pieces[j][:, h : h + 128]
            qpart[k, m, :, 0:n] = exact(ones, acc, NT)[0:1, :]
            qpart[k, m, :, n : n + 128] = inner_sum

            @pl.when(i < C)
            def _():
                push(qpart.at[k, m], sums.at[c], Q_COL[k], (r, m))

            return carry

        lax.fori_loop(1, C + 1, block, 0)
        sums[c] = qpart[k, c]
        arrived(sums, Q_COL[k])
        out = total(sums)
        return out[:, 0:n] + lam * vector, out[:, n : n + 1]

    def reduce_all(row, scalar, k):
        across, along = vrow.at[2 + 2 * k], vcol.at[1 + k]
        across[r, :, 0:rank] = row[0:1, :]
        across[r, :, rank : rank + 128] = wide(scalar)
        spread_row(across, A_ROW[k])
        arrived(across, A_ROW[k])
        along[c] = total(across)
        spread_col(along, A_COL[k])
        arrived(along, A_COL[k])
        out = total(along)
        return out[:, 0:rank], out[:, rank : rank + 1]

    direction = precondition(resid, w)
    image, descent = operate(direction, resid * direction, 0)
    projected, curve = reduce_all(exact(image, sketch_out[...], NN), lanes(direction * image), 0)
    step = descent / curve
    coef = step * direction
    resid = resid - step * image
    precond = precondition(resid, w - step * projected)
    next_image, fresh = operate(precond, resid * precond, 1)
    ratio = fresh / descent
    direction = precond + ratio * direction
    image = next_image + ratio * image
    _, curve = reduce_all(direction, lanes(direction * image), 1)
    step = fresh / curve
    coef_out[...] = (coef + step * direction)[0:1, :]
    resid_out[...] = (resid - step * image)[0:1, :]

    for s in range(2):
        for d in range(A):
            for there, slot in line(d) if d else ((None, r),):
                for condition, move in hops(slot, s):
                    both = [x for x in (there, condition) if x is not None]
                    if both:
                        pl.when(functools.reduce(jnp.logical_and, both))(move.wait_send)
                    else:
                        move.wait_send()
    sent(xcol, X_COL)
    pltpu.make_async_copy(mine, mine, send.at[PAIR]).wait()
    sent(srecv, SKETCH)
    sent(crecv, CORE)
    sent(crow.at[1], CORE_ROW)
    sent(cgath, CORE_ALL)
    sent(call, CORE_COL)
    sent(w_row, W_ROW)
    sent(w_col, W_COL)
    for k in range(2):
        sent(vrow.at[1 + 2 * k], Z_ROW[k])
        sent(qcol.at[k], Q_COL[k])
        sent(vrow.at[2 + 2 * k], A_ROW[k])
        sent(vcol.at[1 + k], A_COL[k])


def local(R, C, points, feature_scale, test_matrix, targets, ridge):
    n, feats = points.shape
    rank = test_matrix.shape[1]
    f32, half = jnp.float32, jnp.bfloat16
    vmem = pl.BlockSpec(memory_space=pltpu.VMEM)
    coef, resid, sketch = pl.pallas_call(
        functools.partial(kernel, R, C),
        out_shape=(
            jax.ShapeDtypeStruct((1, n), f32),
            jax.ShapeDtypeStruct((1, n), f32),
            jax.ShapeDtypeStruct((n, rank), f32),
        ),
        in_specs=[vmem, vmem, vmem, vmem, pl.BlockSpec(memory_space=pltpu.SMEM)],
        out_specs=(vmem, vmem, vmem),
        scratch_shapes=[
            pltpu.VMEM((R, n, 2 * feats), half),
            pltpu.VMEM((R, n, rank), half),
            pltpu.VMEM((C, n, 2 * feats), half),
            pltpu.VMEM((C, n, 4 * feats), half),
            pltpu.VMEM((C, n, 128), f32),
            pltpu.VMEM((R, C, n, n), f32),
            pltpu.VMEM((C, n, rank), f32),
            pltpu.VMEM((C, n, rank), f32),
            pltpu.VMEM((C // CORES, n, rank), f32),
            pltpu.VMEM((C, rank // C, rank), f32),
            pltpu.VMEM((C, rank // C, rank), f32),
            pltpu.VMEM((2, R, rank // C // R, rank), f32),
            pltpu.VMEM((R, rank // C // R, rank), f32),
            pltpu.VMEM((C, rank // C, rank), f32),
            pltpu.VMEM((rank, rank), f32),
            pltpu.VMEM((rank, n), f32),
            pltpu.VMEM((5, R, 1, n + 128), f32),
            pltpu.VMEM((3, C, 1, n + 128), f32),
            pltpu.VMEM((2, C, 1, n + 128), f32),
            pltpu.VMEM((2, C, 1, n + 128), f32),
            pltpu.SemaphoreType.DMA((ROUNDS,)),
            pltpu.SemaphoreType.DMA((ROUNDS,)),
            pltpu.SemaphoreType.DMA((2, R, 6)),
            pltpu.SemaphoreType.DMA((2, R)),
        ],
        compiler_params=pltpu.CompilerParams(
            collective_id=0, has_side_effects=True, vmem_limit_bytes=56 * 1024 * 1024
        ),
    )(points.T, feature_scale.reshape(1, feats), test_matrix, targets.reshape(1, n), ridge.reshape(1, 1))
    return coef.reshape(n), resid.reshape(n), sketch


def solution(mesh):
    R, C = mesh.shape["row"], mesh.shape["col"]
    in_specs = (P(("col", "row"), None), P(), P(("col", "row"), None), P(("col", "row")), P())
    out_specs = (P(("col", "row")), P(("col", "row")), P(("col", "row"), None))
    return jax.shard_map(
        functools.partial(local, R, C), mesh=mesh, in_specs=in_specs, out_specs=out_specs,
        check_vma=False,
    )
```

```python
import functools

import jax
import jax.numpy as jnp
from jax import lax
from jax.experimental import pallas as pl
from jax.experimental.pallas import tpu as pltpu
from jax.sharding import PartitionSpec as P

MESH = pl.DeviceIdType.MESH
EXACT = lax.Precision.HIGHEST
NN = (((1,), (0,)), ((), ()))
NT = (((1,), (1,)), ((), ()))
TN = (((0,), (0,)), ((), ()))
X_COL, PAIR, SKETCH, CORE, CORE_ROW, CORE_ALL, CORE_COL, W_ROW, W_COL, S_ALL = range(10)
Z_ROW, Z_COL, Q_COL, FLAT = (10, 14), (11, 15), (12, 16), (13, 17)
ROUNDS = 18
CORES = 2


def exact(left, right, dims):
    return lax.dot_general(
        left, right, dims, precision=EXACT, preferred_element_type=jnp.float32
    )


def invert(a):
    size, width = a.shape[0], 8
    lane = lax.broadcasted_iota(jnp.int32, a.shape, 1)
    lane_row = lane[0:1, :]

    def pivots(a, k):
        entry = [
            [jnp.broadcast_to(a[k + i : k + i + 1, k + j : k + j + 1], (1, size)) for j in range(width)]
            for i in range(width)
        ]
        rows = [a[k + i : k + i + 1, :] for i in range(width)]
        cols = [a[:, k + i : k + i + 1] for i in range(width)]
        for t in range(0, width, 2):
            p, q, s, u = entry[t][t], entry[t][t + 1], entry[t + 1][t], entry[t + 1][t + 1]
            inverse = 1.0 / (p * u - q * s)
            p, q, s, u = u * inverse, -q * inverse, -s * inverse, p * inverse
            here, next_one = lane_row == k + t, lane_row == k + t + 1
            pair = here | next_one
            one, two = rows[t], rows[t + 1]
            rows[t] = jnp.where(here, p, jnp.where(next_one, q, p * one + q * two))
            rows[t + 1] = jnp.where(here, s, jnp.where(next_one, u, s * one + u * two))
            for j in range(t + 2, width):
                one, two = entry[t][j], entry[t + 1][j]
                entry[t][j], entry[t + 1][j] = p * one + q * two, s * one + u * two
            for i in range(width):
                if i not in (t, t + 1):
                    one, two = entry[i][t], entry[i][t + 1]
                    rows[i] = jnp.where(pair, 0.0, rows[i]) - one * rows[t] - two * rows[t + 1]
                    for j in range(t + 2, width):
                        entry[i][j] = entry[i][j] - one * entry[t][j] - two * entry[t + 1][j]
        out = jnp.where((lane >= k) & (lane < k + width), 0.0, a)
        for t in range(width):
            out = out - cols[t] * rows[t]
        return out, rows

    def turn(_, a):
        a, rows = pivots(a, 0)
        a = jnp.concatenate([a[width:, :]] + rows, axis=0)
        return pltpu.roll(a, size - width, 1)

    return lax.fori_loop(0, size // width, turn, a)


def kernel(
    R, C, pts, scale, test, tgt, ridge, coef_out, resid_out, sketch_out,
    xrow, trow, xcol, left, left_norm, kmat, part, pair, srecv, core, crecv, crow, cgath, call, inv, spread_ref,
    vrow, vcol, zrow, zcol, qpart, qcol, flat, flat_late, srow, send, recv, gather_send, gather_recv,
    pair_send, pair_recv,
):
    r, c = lax.axis_index("row"), lax.axis_index("col")
    feats, n = pts.shape
    rank = test.shape[1]
    chunk = rank // C
    piece = chunk // R
    B = R // 4 if R % 4 == 0 else 1
    A = R // B
    half = rank // 2
    lam = ridge[0, 0]

    def to_row(i):
        return (lax.rem(r + i, R), c)

    def to_col(i):
        return (r, lax.rem(c + i, C))

    def copy(src, dst, out, into, dev):
        return pltpu.make_async_remote_copy(
            src_ref=src, dst_ref=dst, send_sem=out, recv_sem=into,
            device_id=dev, device_id_type=MESH,
        )

    def push(src, dst, k, dev):
        copy(src, dst, send.at[k], recv.at[k], dev).start()

    def spread_row(buf, k):
        for i in range(1, R):
            push(buf.at[r], buf.at[r], k, to_row(i))

    def spread_col(buf, k):
        for i in range(1, C):
            push(buf.at[c], buf.at[c], k, to_col(i))

    everyone = R * C
    me = c * R + r

    def device(i):
        peer = lax.rem(me + i, everyone)
        return (lax.rem(peer, R), lax.div(peer, R))

    def spread_flat(buf, k):
        def one(i, carry):
            push(buf.at[me], buf.at[me], k, device(i))
            return carry

        lax.fori_loop(1, everyone, one, 0)

    def arrived(buf, k):
        part_of = buf.at[pl.ds(0, buf.shape[0] - 1)]
        pltpu.make_async_copy(part_of, part_of, recv.at[k]).wait()

    def sent(buf, k):
        part_of = buf.at[pl.ds(0, buf.shape[0] - 1)]
        pltpu.make_async_copy(part_of, part_of, send.at[k]).wait()

    def total(buf):
        acc = buf[0]
        for i in range(1, buf.shape[0]):
            acc = acc + buf[i]
        return acc

    barrier = pltpu.get_barrier_semaphore()

    def greet(i, carry):
        pl.semaphore_signal(barrier, inc=1, device_id=device(i), device_id_type=MESH)
        return carry

    lax.fori_loop(1, everyone, greet, 0)

    scaled = pts[...].T * scale[...]
    high = scaled.astype(jnp.bfloat16).astype(jnp.float32)
    both = jnp.concatenate([high, scaled - high], axis=1).astype(jnp.bfloat16)
    xrow[r] = both
    xcol[c] = both
    trow[r] = test[...]
    part[...] = jnp.zeros_like(part)
    pl.semaphore_wait(barrier, everyone - 1)
    spread_col(xcol, X_COL)

    along, across = lax.div(r, B), lax.rem(r, B)
    stores = (xrow, trow)

    def hops(slot, s):
        origin = lax.div(slot, B)

        def make(kind, dev):
            return copy(
                stores[s].at[slot], stores[s].at[slot], gather_send.at[s, slot, kind],
                gather_recv.at[s, slot], (dev, c),
            )

        out = [
            ((origin <= along) & (along + 1 < A), make(0, lax.rem(r + B, R))),
            ((origin >= along) & (along >= 1), make(1, lax.rem(r + R - B, R))),
        ]
        for i in range(1, B):
            out.append((None, make(1 + i, along * B + lax.rem(across + i, B))))
        return out

    def forward(slot, s):
        for condition, move in hops(slot, s):
            if condition is None:
                move.start()
            else:
                pl.when(condition)(move.start)

    def landed(slot, s):
        here = stores[s].at[slot]
        pltpu.make_async_copy(here, here, gather_recv.at[s, slot]).wait()

    ones = jnp.ones((8, 128), jnp.float32)

    def pair_sum(x):
        swapped = pltpu.roll(x, feats, 1)
        return swapped, x * (x + swapped)

    def consume(slot):
        y = xrow[slot]
        right_norm = -0.5 * exact(ones, pair_sum(y.astype(jnp.float32))[1], NT)[0:1, :]
        cross = lax.dot_general(
            left[...].reshape(C * n, 4 * feats), jnp.concatenate([y, y], axis=1), NT,
            preferred_element_type=jnp.float32,
        )
        norm = left_norm[...].reshape(C * n, 128)
        weights = jnp.exp(cross + jnp.concatenate([norm] * (n // 128), axis=1) + right_norm)
        kmat[slot] = weights.reshape(C, n, n)
        term = lax.dot_general(
            weights.astype(jnp.bfloat16), trow[slot], NN, preferred_element_type=jnp.float32
        )
        part[...] = part[...] + term.reshape(C, n, rank)

    for s in range(2):
        forward(r, s)
    arrived(xcol, X_COL)
    for m in range(C):
        x = xcol[m]
        swapped, square = pair_sum(x.astype(jnp.float32))
        left[m] = jnp.concatenate([x, swapped.astype(jnp.bfloat16)], axis=1)
        left_norm[m] = jnp.broadcast_to(-0.5 * jnp.sum(square, axis=1, keepdims=True), (n, 128))

    consume(r)

    def sides(distance, action, line_of):
        def one(side, carry):
            position = along + distance * (2 * side - 1)

            @pl.when((position >= 0) & (position < A) & ((distance > 0) | (side > 0)))
            def _():
                action(position * B + line_of)

            return carry

        lax.fori_loop(0, 2, one, 0)

    def receive(slot):
        for s in range(2):
            landed(slot, s)
            forward(slot, s)

    def crossed(slot):
        for s in range(2):
            landed(slot, s)
        consume(slot)

    def level(d, carry):
        sides(d, receive, across)
        sides(d, consume, across)

        def other(i, inner):
            sides(d - 1, crossed, lax.rem(across + i, B))
            return inner

        lax.fori_loop(1, B, other, 0)
        return carry

    lax.fori_loop(1, A + 1, level, 0)

    chip, side = lax.div(c, CORES), lax.rem(c, CORES)
    chips = C // CORES
    for i in range(chips):
        m = lax.rem(chip + 1 + i, chips) * CORES + 1 - side
        copy(
            part.at[m], pair.at[m - 1 + side], pair_send.at[i], pair_recv.at[i],
            (r, chip * CORES + 1 - side),
        ).start()
    for i in range(chips):
        m = lax.rem(chip + 1 + i, chips)
        pltpu.make_async_copy(pair.at[0], pair.at[0], pair_recv.at[i]).wait()
        summed = part[m * CORES + side] + pair[m * CORES]
        if i < chips - 1:
            part[m * CORES + side] = summed
            push(part.at[m * CORES + side], srecv.at[chip], SKETCH, (r, m * CORES + side))
        else:
            srecv[chip] = summed
    arrived(srecv, SKETCH)
    sketch = total(srecv)
    sketch_out[...] = sketch

    resid = jnp.broadcast_to(tgt[...], (8, n))
    local = exact(lam * test[...].astype(jnp.float32) + sketch, sketch, TN)
    for i in range(C):
        core[i] = local[i * chunk : (i + 1) * chunk, :]
    for i in range(1, C):
        push(core.at[lax.rem(c + i, C)], crecv.at[c], CORE, to_col(i))
    w_row, w_col = vrow, vcol
    w_row[r] = exact(resid, sketch, NN)[0:1, :]
    spread_row(w_row, W_ROW)
    crecv[c] = core[c]
    arrived(crecv, CORE)
    summed = total(crecv)
    for i in range(R):
        crow[0, i] = summed[i * piece : (i + 1) * piece, :]
    for i in range(1, R):
        push(crow.at[0, lax.rem(r + i, R)], crow.at[1, r], CORE_ROW, to_row(i))
    arrived(w_row, W_ROW)
    w_col[c] = total(w_row)
    spread_col(w_col, W_COL)
    crow[1, r] = crow[0, r]
    arrived(crow.at[1], CORE_ROW)
    cgath[r] = total(crow.at[1])
    spread_row(cgath, CORE_ALL)
    arrived(cgath, CORE_ALL)
    call[c] = cgath[...].reshape(chunk, rank)
    spread_col(call, CORE_COL)
    srow[c] = sketch
    spread_col(srow, S_ALL)
    arrived(w_col, W_COL)
    w = total(w_col)
    arrived(call, CORE_COL)

    whole = call[...].reshape(rank, rank)
    top, up = whole[:half, :half], whole[:half, half:]
    down, low = whole[half:, :half], whole[half:, half:]
    first = invert(top)
    above = exact(first, up, NN)
    below = exact(down, first, NN)
    second = invert(low - exact(down, above, NN))
    corner = exact(second, below, NN)
    inv[:half, :half] = first + exact(above, corner, NN)
    inv[:half, half:] = -exact(above, second, NN)
    inv[half:, :half] = -corner
    inv[half:, half:] = second

    spread_ref[...] = exact(inv[...], sketch, NT)

    def lanes(x):
        return jnp.sum(x, axis=1, keepdims=True)

    tag = lax.broadcasted_iota(jnp.int32, (1, 128), 1)

    def precondition(resid, w):
        return (resid - exact(jnp.broadcast_to(w, (8, rank)), spread_ref[...], NN)) / lam

    def operate(vector, extras, k):
        first = k == 0
        across, along, sums = zrow.at[k], zcol.at[k], qcol.at[k]
        across[r] = vector[0:1, :]
        along[c] = vector[0:1, :]
        spread_row(across, Z_ROW[k])
        spread_col(along, Z_COL[k])
        own = lam * vector[0:1, :]
        scalars = [lanes(own * vector[0:1, :])] + [lanes(x[0:1, :]) for x in extras]
        if first:
            projected = lam * exact(vector, sketch_out[...], NN)[0:1, :]
            folded = jnp.zeros((8, rank), jnp.float32)
            arrived(srow, S_ALL)
        arrived(across, Z_ROW[k])
        pieces = [across[j] for j in range(R)]
        arrived(along, Z_COL[k])
        for i in range(1, C + 1):
            m = lax.rem(c + i, C)
            acc = jnp.zeros((n, 128), jnp.float32)
            for j in range(R):
                for h in range(0, n, 128):
                    acc += kmat[j, m, :, h : h + 128] * pieces[j][:, h : h + 128]
            row = exact(ones, acc, NT)[0:1, :]
            if i < C:
                qpart[k, m] = row
                push(qpart.at[k, m], sums.at[c], Q_COL[k], (r, m))
            else:
                sums[c] = row + own
            scalars[0] += lanes(row * along[m])
            if first:
                folded += jnp.sum((lanes(acc) * srow[m]).reshape(n // 8, 8, rank), axis=0)
        packed = jnp.zeros((1, 128), jnp.float32)
        for i, x in enumerate(scalars):
            packed = jnp.where(tag == i, x, packed)
        shared = flat if first else flat_late
        if first:
            shared[me, :, 128 : 128 + rank] = projected + jnp.sum(folded, axis=0, keepdims=True)
        shared[me, :, 0:128] = packed
        spread_flat(shared, FLAT[k])
        arrived(sums, Q_COL[k])
        image = total(sums)
        arrived(shared, FLAT[k])
        out = total(shared)
        return image, [out[:, i : i + 1] for i in range(len(scalars))], out[:, 128:]

    direction = precondition(resid, w)
    image, (curve, descent), projected = operate(direction, [resid * direction], 0)
    step = descent / curve
    coef = step * direction
    resid = resid - step * image
    precond = precondition(resid, w - step * projected)
    late, (late_curve, fresh, mixed), _ = operate(precond, [resid * precond, precond * image], 1)
    ratio = fresh / descent
    direction = precond + ratio * direction
    image = late + ratio * image
    step = fresh / (late_curve + ratio * (2.0 * mixed + ratio * curve))
    coef_out[...] = (coef + step * direction)[0:1, :]
    resid_out[...] = (resid - step * image)[0:1, :]

    def line(d):
        return ((along >= d, r - d * B), (along + d < A, r + d * B))

    for s in range(2):
        for d in range(A):
            for there, slot in line(d) if d else ((None, r),):
                for condition, move in hops(slot, s):
                    both = [x for x in (there, condition) if x is not None]
                    if both:
                        pl.when(functools.reduce(jnp.logical_and, both))(move.wait_send)
                    else:
                        move.wait_send()
    sent(xcol, X_COL)
    for i in range(chips):
        pltpu.make_async_copy(pair.at[0], pair.at[0], pair_send.at[i]).wait()
    sent(srecv, SKETCH)
    sent(crecv, CORE)
    sent(crow.at[1], CORE_ROW)
    sent(cgath, CORE_ALL)
    sent(call, CORE_COL)
    sent(w_row, W_ROW)
    sent(w_col, W_COL)
    sent(srow, S_ALL)
    for k in range(2):
        sent(zrow.at[k], Z_ROW[k])
        sent(zcol.at[k], Z_COL[k])
        sent(qcol.at[k], Q_COL[k])
        sent((flat, flat_late)[k], FLAT[k])


def local(R, C, points, feature_scale, test_matrix, targets, ridge):
    n, feats = points.shape
    rank = test_matrix.shape[1]
    f32, half = jnp.float32, jnp.bfloat16
    vmem = pl.BlockSpec(memory_space=pltpu.VMEM)
    coef, resid, sketch = pl.pallas_call(
        functools.partial(kernel, R, C),
        out_shape=(
            jax.ShapeDtypeStruct((1, n), f32),
            jax.ShapeDtypeStruct((1, n), f32),
            jax.ShapeDtypeStruct((n, rank), f32),
        ),
        in_specs=[vmem, vmem, vmem, vmem, pl.BlockSpec(memory_space=pltpu.SMEM)],
        out_specs=(vmem, vmem, vmem),
        scratch_shapes=[
            pltpu.VMEM((R, n, 2 * feats), half),
            pltpu.VMEM((R, n, rank), half),
            pltpu.VMEM((C, n, 2 * feats), half),
            pltpu.VMEM((C, n, 4 * feats), half),
            pltpu.VMEM((C, n, 128), f32),
            pltpu.VMEM((R, C, n, n), f32),
            pltpu.VMEM((C, n, rank), f32),
            pltpu.VMEM((C, n, rank), f32),
            pltpu.VMEM((C // CORES, n, rank), f32),
            pltpu.VMEM((C, rank // C, rank), f32),
            pltpu.VMEM((C, rank // C, rank), f32),
            pltpu.VMEM((2, R, rank // C // R, rank), f32),
            pltpu.VMEM((R, rank // C // R, rank), f32),
            pltpu.VMEM((C, rank // C, rank), f32),
            pltpu.VMEM((rank, rank), f32),
            pltpu.VMEM((rank, n), f32),
            pltpu.VMEM((R, 1, rank), f32),
            pltpu.VMEM((C, 1, rank), f32),
            pltpu.VMEM((2, R, 1, n), f32),
            pltpu.VMEM((2, C, 1, n), f32),
            pltpu.VMEM((2, C, 1, n), f32),
            pltpu.VMEM((2, C, 1, n), f32),
            pltpu.VMEM((R * C, 1, 128 + rank), f32),
            pltpu.VMEM((R * C, 1, 128), f32),
            pltpu.VMEM((C, n, rank), f32),
            pltpu.SemaphoreType.DMA((ROUNDS,)),
            pltpu.SemaphoreType.DMA((ROUNDS,)),
            pltpu.SemaphoreType.DMA((2, R, 6)),
            pltpu.SemaphoreType.DMA((2, R)),
            pltpu.SemaphoreType.DMA((C,)),
            pltpu.SemaphoreType.DMA((C,)),
        ],
        compiler_params=pltpu.CompilerParams(
            collective_id=0, has_side_effects=True, vmem_limit_bytes=56 * 1024 * 1024
        ),
    )(points.T, feature_scale.reshape(1, feats), test_matrix, targets.reshape(1, n), ridge.reshape(1, 1))
    return coef.reshape(n), resid.reshape(n), sketch


def solution(mesh):
    R, C = mesh.shape["row"], mesh.shape["col"]
    in_specs = (P(("col", "row"), None), P(), P(("col", "row"), None), P(("col", "row")), P())
    out_specs = (P(("col", "row")), P(("col", "row")), P(("col", "row"), None))
    return jax.shard_map(
        functools.partial(local, R, C), mesh=mesh, in_specs=in_specs, out_specs=out_specs,
        check_vma=False,
    )
```

```python
import functools

import jax
import jax.numpy as jnp
from jax import lax
from jax.experimental import pallas as pl
from jax.experimental.pallas import tpu as pltpu
from jax.sharding import PartitionSpec as P

MESH = pl.DeviceIdType.MESH
EXACT = lax.Precision.HIGHEST
NN = (((1,), (0,)), ((), ()))
NT = (((1,), (1,)), ((), ()))
TN = (((0,), (0,)), ((), ()))
X_COL, PAIR, SKETCH, CORE, CORE_ROW, CORE_ALL, CORE_COL, W_ROW, W_COL, S_ALL = range(10)
Z_ROW, Z_COL, Q_COL, FLAT = (10, 14), (11, 15), (12, 16), (13, 17)
ROUNDS = 18
CORES = 2
BANDS = 4


def exact(left, right, dims):
    return lax.dot_general(
        left, right, dims, precision=EXACT, preferred_element_type=jnp.float32
    )


def invert(a):
    size, width = a.shape[0], 8
    lane = lax.broadcasted_iota(jnp.int32, a.shape, 1)
    lane_row = lane[0:1, :]

    def pivots(a, k):
        entry = [
            [jnp.broadcast_to(a[k + i : k + i + 1, k + j : k + j + 1], (1, size)) for j in range(width)]
            for i in range(width)
        ]
        rows = [a[k + i : k + i + 1, :] for i in range(width)]
        cols = [a[:, k + i : k + i + 1] for i in range(width)]
        for t in range(0, width, 2):
            p, q, s, u = entry[t][t], entry[t][t + 1], entry[t + 1][t], entry[t + 1][t + 1]
            inverse = 1.0 / (p * u - q * s)
            p, q, s, u = u * inverse, -q * inverse, -s * inverse, p * inverse
            here, next_one = lane_row == k + t, lane_row == k + t + 1
            pair = here | next_one
            one, two = rows[t], rows[t + 1]
            rows[t] = jnp.where(here, p, jnp.where(next_one, q, p * one + q * two))
            rows[t + 1] = jnp.where(here, s, jnp.where(next_one, u, s * one + u * two))
            for j in range(t + 2, width):
                one, two = entry[t][j], entry[t + 1][j]
                entry[t][j], entry[t + 1][j] = p * one + q * two, s * one + u * two
            for i in range(width):
                if i not in (t, t + 1):
                    one, two = entry[i][t], entry[i][t + 1]
                    rows[i] = jnp.where(pair, 0.0, rows[i]) - one * rows[t] - two * rows[t + 1]
                    for j in range(t + 2, width):
                        entry[i][j] = entry[i][j] - one * entry[t][j] - two * entry[t + 1][j]
        out = jnp.where((lane >= k) & (lane < k + width), 0.0, a)
        for t in range(width):
            out = out - cols[t] * rows[t]
        return out, rows

    def turn(_, a):
        a, rows = pivots(a, 0)
        a = jnp.concatenate([a[width:, :]] + rows, axis=0)
        return pltpu.roll(a, size - width, 1)

    return lax.fori_loop(0, size // width, turn, a)


def kernel(
    R, C, pts, scale, test, tgt, ridge, both_out, sketch_out,
    xrow, trow, xcol, left, left_norm, kmat, part, pair, srecv, core, crecv, crow, cgath, call, inv, spread_ref,
    vrow, vcol, zrow, zcol, qpart, qcol, flat, flat_late, srow, send, recv, gather_send, gather_recv,
    pair_send, pair_recv,
):
    r, c = lax.axis_index("row"), lax.axis_index("col")
    feats, n = pts.shape
    rank = test.shape[1]
    chunk = rank // C
    piece = chunk // R
    B = R // 4 if R % 4 == 0 else 1
    A = R // B
    half = rank // 2
    lam = ridge[0, 0]

    def to_row(i):
        return (lax.rem(r + i, R), c)

    def to_col(i):
        return (r, lax.rem(c + i, C))

    def copy(src, dst, out, into, dev):
        return pltpu.make_async_remote_copy(
            src_ref=src, dst_ref=dst, send_sem=out, recv_sem=into,
            device_id=dev, device_id_type=MESH,
        )

    def push(src, dst, k, dev):
        copy(src, dst, send.at[k], recv.at[k], dev).start()

    def spread_row(buf, k):
        for i in range(1, R):
            push(buf.at[r], buf.at[r], k, to_row(i))

    def spread_col(buf, k):
        for i in range(1, C):
            push(buf.at[c], buf.at[c], k, to_col(i))

    everyone = R * C
    me = c * R + r

    def device(i):
        peer = lax.rem(me + i, everyone)
        return (lax.rem(peer, R), lax.div(peer, R))

    def spread_flat(buf, k):
        def one(i, carry):
            push(buf.at[me], buf.at[me], k, device(i))
            return carry

        lax.fori_loop(1, everyone, one, 0)

    def arrived(buf, k):
        part_of = buf.at[pl.ds(0, buf.shape[0] - 1)]
        pltpu.make_async_copy(part_of, part_of, recv.at[k]).wait()

    def sent(buf, k):
        part_of = buf.at[pl.ds(0, buf.shape[0] - 1)]
        pltpu.make_async_copy(part_of, part_of, send.at[k]).wait()

    def total(buf):
        acc = buf[0]
        for i in range(1, buf.shape[0]):
            acc = acc + buf[i]
        return acc

    barrier = pltpu.get_barrier_semaphore()

    def greet(i, carry):
        pl.semaphore_signal(barrier, inc=1, device_id=device(i), device_id_type=MESH)
        return carry

    lax.fori_loop(1, everyone, greet, 0)

    scaled = pts[...].T * scale[...]
    high = scaled.astype(jnp.bfloat16).astype(jnp.float32)
    both = jnp.concatenate([high, scaled - high], axis=1).astype(jnp.bfloat16)
    xrow[r] = both
    xcol[c] = both
    trow[r] = test[...]
    part[...] = jnp.zeros_like(part)
    pl.semaphore_wait(barrier, everyone - 1)
    spread_col(xcol, X_COL)

    along, across = lax.div(r, B), lax.rem(r, B)
    stores = (xrow, trow)

    def hops(slot, s):
        origin = lax.div(slot, B)

        def make(kind, dev):
            return copy(
                stores[s].at[slot], stores[s].at[slot], gather_send.at[s, slot, kind],
                gather_recv.at[s, slot], (dev, c),
            )

        out = [
            ((origin <= along) & (along + 1 < A), make(0, lax.rem(r + B, R))),
            ((origin >= along) & (along >= 1), make(1, lax.rem(r + R - B, R))),
        ]
        for i in range(1, B):
            out.append((None, make(1 + i, along * B + lax.rem(across + i, B))))
        return out

    def forward(slot, s):
        for condition, move in hops(slot, s):
            if condition is None:
                move.start()
            else:
                pl.when(condition)(move.start)

    def landed(slot, s):
        here = stores[s].at[slot]
        pltpu.make_async_copy(here, here, gather_recv.at[s, slot]).wait()

    ones = jnp.ones((8, 128), jnp.float32)

    def pair_sum(x):
        swapped = pltpu.roll(x, feats, 1)
        return swapped, x * (x + swapped)

    def consume(slot):
        y = xrow[slot]
        right_norm = -0.5 * exact(ones, pair_sum(y.astype(jnp.float32))[1], NT)[0:1, :]
        cross = lax.dot_general(
            left[...].reshape(C * n, 4 * feats), jnp.concatenate([y, y], axis=1), NT,
            preferred_element_type=jnp.float32,
        )
        norm = left_norm[...].reshape(C * n, 128)
        weights = jnp.exp(cross + jnp.concatenate([norm] * (n // 128), axis=1) + right_norm)
        kmat[slot] = weights.reshape(C, n, n)
        term = lax.dot_general(
            weights.astype(jnp.bfloat16), trow[slot], NN, preferred_element_type=jnp.float32
        )
        part[...] = part[...] + term.reshape(C, n, rank)

    for s in range(2):
        forward(r, s)
    arrived(xcol, X_COL)
    for m in range(C):
        x = xcol[m]
        swapped, square = pair_sum(x.astype(jnp.float32))
        left[m] = jnp.concatenate([x, swapped.astype(jnp.bfloat16)], axis=1)
        left_norm[m] = jnp.broadcast_to(-0.5 * jnp.sum(square, axis=1, keepdims=True), (n, 128))

    consume(r)

    def sides(distance, action, line_of):
        def one(side, carry):
            position = along + distance * (2 * side - 1)

            @pl.when((position >= 0) & (position < A) & ((distance > 0) | (side > 0)))
            def _():
                action(position * B + line_of)

            return carry

        lax.fori_loop(0, 2, one, 0)

    def receive(slot):
        for s in range(2):
            landed(slot, s)
            forward(slot, s)

    def crossed(slot):
        for s in range(2):
            landed(slot, s)
        consume(slot)

    def level(d, carry):
        sides(d, receive, across)
        sides(d, consume, across)

        def other(i, inner):
            sides(d - 1, crossed, lax.rem(across + i, B))
            return inner

        lax.fori_loop(1, B, other, 0)
        return carry

    lax.fori_loop(1, A + 1, level, 0)

    chip, side = lax.div(c, CORES), lax.rem(c, CORES)
    chips = C // CORES
    bands = [pl.ds(h * (n // BANDS), n // BANDS) for h in range(BANDS)]
    for i in range(chips):
        m = lax.rem(chip + 1 + i, chips) * CORES + 1 - side
        for h, band in enumerate(bands):
            copy(
                part.at[m, band], pair.at[m - 1 + side, band], pair_send.at[i, h], pair_recv.at[i, h],
                (r, chip * CORES + 1 - side),
            ).start()
    for i in range(chips):
        m = lax.rem(chip + 1 + i, chips)
        for h, band in enumerate(bands):
            here = pair.at[0, band]
            pltpu.make_async_copy(here, here, pair_recv.at[i, h]).wait()
            summed = part[m * CORES + side, band] + pair[m * CORES, band]
            if i < chips - 1:
                part[m * CORES + side, band] = summed
                push(
                    part.at[m * CORES + side, band], srecv.at[chip, band], SKETCH,
                    (r, m * CORES + side),
                )
            else:
                srecv[chip, band] = summed
    arrived(srecv, SKETCH)
    sketch = total(srecv)
    sketch_out[...] = sketch

    resid = jnp.broadcast_to(tgt[...], (8, n))
    local = exact(lam * test[...].astype(jnp.float32) + sketch, sketch, TN)
    for i in range(C):
        core[i] = local[i * chunk : (i + 1) * chunk, :]
    for i in range(1, C):
        push(core.at[lax.rem(c + i, C)], crecv.at[c], CORE, to_col(i))
    w_row, w_col = vrow, vcol
    w_row[r] = exact(resid, sketch, NN)[0:1, :]
    spread_row(w_row, W_ROW)
    crecv[c] = core[c]
    arrived(crecv, CORE)
    summed = total(crecv)
    for i in range(R):
        crow[0, i] = summed[i * piece : (i + 1) * piece, :]
    for i in range(1, R):
        push(crow.at[0, lax.rem(r + i, R)], crow.at[1, r], CORE_ROW, to_row(i))
    arrived(w_row, W_ROW)
    w_col[c] = total(w_row)
    spread_col(w_col, W_COL)
    crow[1, r] = crow[0, r]
    arrived(crow.at[1], CORE_ROW)
    cgath[r] = total(crow.at[1])
    spread_row(cgath, CORE_ALL)
    arrived(cgath, CORE_ALL)
    call[c] = cgath[...].reshape(chunk, rank)
    spread_col(call, CORE_COL)
    srow[c] = sketch
    spread_col(srow, S_ALL)
    arrived(w_col, W_COL)
    w = total(w_col)
    arrived(call, CORE_COL)

    whole = call[...].reshape(rank, rank)
    top, up = whole[:half, :half], whole[:half, half:]
    down, low = whole[half:, :half], whole[half:, half:]
    first = invert(top)
    above = exact(first, up, NN)
    below = exact(down, first, NN)
    second = invert(low - exact(down, above, NN))
    corner = exact(second, below, NN)
    inv[:half, :half] = first + exact(above, corner, NN)
    inv[:half, half:] = -exact(above, second, NN)
    inv[half:, :half] = -corner
    inv[half:, half:] = second

    spread = exact(inv[...], sketch, NT)
    left_over = sketch.T - exact(call[...].reshape(rank, rank), spread, NN)
    spread_ref[...] = spread + exact(inv[...], left_over, NN)

    def lanes(x):
        return jnp.sum(x, axis=1, keepdims=True)

    tag = lax.broadcasted_iota(jnp.int32, (1, 128), 1)

    def precondition(resid, w):
        return (resid - exact(jnp.broadcast_to(w, (8, rank)), spread_ref[...], NN)) / lam

    def operate(vector, extras, k):
        first = k == 0
        across, along, sums = zrow.at[k], zcol.at[k], qcol.at[k]
        across[r] = vector[0:1, :]
        along[c] = vector[0:1, :]
        spread_row(across, Z_ROW[k])
        spread_col(along, Z_COL[k])
        own = lam * vector[0:1, :]
        scalars = [lanes(own * vector[0:1, :])] + [lanes(x[0:1, :]) for x in extras]
        if first:
            projected = lam * exact(vector, sketch_out[...], NN)[0:1, :]
            folded = jnp.zeros((8, rank), jnp.float32)
            arrived(srow, S_ALL)
        arrived(across, Z_ROW[k])
        pieces = [across[j] for j in range(R)]
        arrived(along, Z_COL[k])
        for i in range(1, C + 1):
            m = lax.rem(c + i, C)
            acc = jnp.zeros((n, 128), jnp.float32)
            for j in range(R):
                for h in range(0, n, 128):
                    acc += kmat[j, m, :, h : h + 128] * pieces[j][:, h : h + 128]
            row = exact(ones, acc, NT)[0:1, :]
            if i < C:
                qpart[k, m] = row
                push(qpart.at[k, m], sums.at[c], Q_COL[k], (r, m))
            else:
                sums[c] = row + own
            scalars[0] += lanes(row * along[m])
            if first:
                folded += jnp.sum((lanes(acc) * srow[m]).reshape(n // 8, 8, rank), axis=0)
        packed = jnp.zeros((1, 128), jnp.float32)
        for i, x in enumerate(scalars):
            packed = jnp.where(tag == i, x, packed)
        shared = flat if first else flat_late
        if first:
            shared[me, :, 128 : 128 + rank] = projected + jnp.sum(folded, axis=0, keepdims=True)
        shared[me, :, 0:128] = packed
        spread_flat(shared, FLAT[k])
        arrived(sums, Q_COL[k])
        image = total(sums)
        arrived(shared, FLAT[k])
        out = total(shared)
        return image, [out[:, i : i + 1] for i in range(len(scalars))], out[:, 128:]

    direction = precondition(resid, w)
    image, (curve, descent), projected = operate(direction, [resid * direction], 0)
    step = descent / curve
    coef = step * direction
    resid = resid - step * image
    precond = precondition(resid, w - step * projected)
    late, (late_curve, fresh, mixed), _ = operate(precond, [resid * precond, precond * image], 1)
    ratio = fresh / descent
    direction = precond + ratio * direction
    image = late + ratio * image
    step = fresh / (late_curve + ratio * (2.0 * mixed + ratio * curve))
    both_out[:, 0:n] = (coef + step * direction)[0:1, :]
    both_out[:, n : 2 * n] = (resid - step * image)[0:1, :]

    def line(d):
        return ((along >= d, r - d * B), (along + d < A, r + d * B))

    for s in range(2):
        for d in range(A):
            for there, slot in line(d) if d else ((None, r),):
                for condition, move in hops(slot, s):
                    both = [x for x in (there, condition) if x is not None]
                    if both:
                        pl.when(functools.reduce(jnp.logical_and, both))(move.wait_send)
                    else:
                        move.wait_send()
    sent(xcol, X_COL)
    for i in range(chips):
        for h, band in enumerate(bands):
            here = pair.at[0, band]
            pltpu.make_async_copy(here, here, pair_send.at[i, h]).wait()
    sent(srecv, SKETCH)
    sent(crecv, CORE)
    sent(crow.at[1], CORE_ROW)
    sent(cgath, CORE_ALL)
    sent(call, CORE_COL)
    sent(w_row, W_ROW)
    sent(w_col, W_COL)
    sent(srow, S_ALL)
    for k in range(2):
        sent(zrow.at[k], Z_ROW[k])
        sent(zcol.at[k], Z_COL[k])
        sent(qcol.at[k], Q_COL[k])
        sent((flat, flat_late)[k], FLAT[k])


def local(R, C, points, feature_scale, test_matrix, targets, ridge):
    n, feats = points.shape
    rank = test_matrix.shape[1]
    f32, half = jnp.float32, jnp.bfloat16
    vmem = pl.BlockSpec(memory_space=pltpu.VMEM)
    both, sketch = pl.pallas_call(
        functools.partial(kernel, R, C),
        out_shape=(
            jax.ShapeDtypeStruct((1, 2 * n), f32),
            jax.ShapeDtypeStruct((n, rank), f32),
        ),
        in_specs=[vmem, vmem, vmem, vmem, pl.BlockSpec(memory_space=pltpu.SMEM)],
        out_specs=(vmem, vmem),
        scratch_shapes=[
            pltpu.VMEM((R, n, 2 * feats), half),
            pltpu.VMEM((R, n, rank), half),
            pltpu.VMEM((C, n, 2 * feats), half),
            pltpu.VMEM((C, n, 4 * feats), half),
            pltpu.VMEM((C, n, 128), f32),
            pltpu.VMEM((R, C, n, n), f32),
            pltpu.VMEM((C, n, rank), f32),
            pltpu.VMEM((C, n, rank), f32),
            pltpu.VMEM((C // CORES, n, rank), f32),
            pltpu.VMEM((C, rank // C, rank), f32),
            pltpu.VMEM((C, rank // C, rank), f32),
            pltpu.VMEM((2, R, rank // C // R, rank), f32),
            pltpu.VMEM((R, rank // C // R, rank), f32),
            pltpu.VMEM((C, rank // C, rank), f32),
            pltpu.VMEM((rank, rank), f32),
            pltpu.VMEM((rank, n), f32),
            pltpu.VMEM((R, 1, rank), f32),
            pltpu.VMEM((C, 1, rank), f32),
            pltpu.VMEM((2, R, 1, n), f32),
            pltpu.VMEM((2, C, 1, n), f32),
            pltpu.VMEM((2, C, 1, n), f32),
            pltpu.VMEM((2, C, 1, n), f32),
            pltpu.VMEM((R * C, 1, 128 + rank), f32),
            pltpu.VMEM((R * C, 1, 128), f32),
            pltpu.VMEM((C, n, rank), f32),
            pltpu.SemaphoreType.DMA((ROUNDS,)),
            pltpu.SemaphoreType.DMA((ROUNDS,)),
            pltpu.SemaphoreType.DMA((2, R, 6)),
            pltpu.SemaphoreType.DMA((2, R)),
            pltpu.SemaphoreType.DMA((C, BANDS)),
            pltpu.SemaphoreType.DMA((C, BANDS)),
        ],
        compiler_params=pltpu.CompilerParams(
            collective_id=0, has_side_effects=True, vmem_limit_bytes=56 * 1024 * 1024
        ),
    )(points.T, feature_scale.reshape(1, feats), test_matrix, targets.reshape(1, n), ridge.reshape(1, 1))
    return both[0, :n], both[0, n:], sketch


def solution(mesh):
    R, C = mesh.shape["row"], mesh.shape["col"]
    in_specs = (P(("col", "row"), None), P(), P(("col", "row"), None), P(("col", "row")), P())
    out_specs = (P(("col", "row")), P(("col", "row")), P(("col", "row"), None))
    return jax.shard_map(
        functools.partial(local, R, C), mesh=mesh, in_specs=in_specs, out_specs=out_specs,
        check_vma=False,
    )
```
